32 devices in a mesh: groups: 2 (over y), dp: 4 (over z), tensor: 4 (over x, core).
Axes of the slice: x: 2, y: 2, z: 4, core: 2. Of those that a mesh axis runs over, the one named last changes fastest.
Arguments:
- output_gradient: bfloat16 [1024, 15872], P(('groups', 'dp'), 'tensor'), parts along dimension 0, may hold values from -6 to 6
- saved_layer_input: bfloat16 [1024, 14848], P(('groups', 'dp'), 'tensor'), parts along dimension 0, may hold values from -6 to 6
- adapter_middle: bfloat16 [1024, 64], P(('groups', 'dp')), parts along dimension 0, may hold values from -6 to 6
- frozen_weight: bfloat16 [14848, 15872], P('dp', 'tensor'), may hold values from -0.046875 to 0.046875
- block_row_scale: float32 [232, 15872], P('dp', 'tensor'), may hold values from 0.25 to 4
- adapter_down_weight: bfloat16 [8, 64, 14848], P('groups', None, 'dp'), parts along dimension 0, may hold values from -0.375 to 0.375
- adapter_up_weight: bfloat16 [8, 64, 15872], P('groups', None, 'tensor'), parts along dimension 0, may hold values from -0.046875 to 0.046875
- document_lengths: int32 [8, 4], P('groups'), parts along dimension 0, may hold values from 1 to 64, 128 in all within a row
- document_adapter: int32 [8, 4], P('groups'), parts along dimension 0, may hold values from 0 to 3, as said below
- adapter_out_row: int32 [8], P('groups'), parts along dimension 0, may hold values from 0 to 3, each once
Outputs:
- input_grad: bfloat16 [1024, 14848], P(('groups', 'tensor'), 'dp'), parts along dimension 0
- grad_down: float32 [8, 64, 14848], P(('groups', 'dp'), None, 'tensor'), parts along dimension 0
- grad_up: float32 [8, 64, 15872], P(('groups', 'dp'), None, 'tensor'), parts along dimension 0
The draws below stay inside these ranges and needn't reach their ends.
There are 2 independent parts, one for each index of `groups`. The reference program is written for one: setup_inputs(seed, part) draws one part's arguments, and reference() takes and returns one part's arrays. A program takes and returns all parts, laid end to end along the dimension named above; an argument that names none is the same for every part. Nothing has to cross between parts.
Inputs may be any that keep to these rules, and one draw needn't show every extreme that they name: `document_lengths`: each row holds the lengths of the 4 documents packed in order into one block of 128 tokens; a row sums to 128. `document_adapter`: the adapter of each document; the 4 documents of one block have distinct adapters. `adapter_out_row`: a permutation; row adapter_out_row[a] of the gradients belongs to adapter a and is owned by index adapter_out_row[a] // 1 of dp.
All inputs are finite; a program needn't handle non-finite values.
Results may differ from the reference program's by a relative error of at most 0.017.
Values may be sent and summed in bfloat16 or wider, within the bound.
A program may use at most 192 MiB of HBM per device.

```python
import math
import jax
import jax.numpy as jnp
import numpy as np
from jax import lax

MODEL_WIDTH = 14848
JOINED_OUTPUTS = 15872
ADAPTER_RANK = 64
BLK = 64
TOKENS_PER_SHARD = 128
SEGS = 4
MOST = 64
PACKED_TOKENS = 512
ADAPTER_COUNT = 4
N_DP = 4
N_TENSOR = 4


def draw_document_adapter(key, part):
    key = jax.random.fold_in(key, 11)
    base = jax.random.randint(key, (N_DP, ADAPTER_COUNT), 0, 2 ** 20)
    ids = jnp.arange(ADAPTER_COUNT, dtype=jnp.int32)
    score_values = base * ADAPTER_COUNT + ids[None, :]
    forced = (jnp.arange(N_DP, dtype=jnp.int32)[:, None] == 0) & ((ids == 0) | (ids == ADAPTER_COUNT - 1))[None, :]
    score_values = score_values - jnp.where(forced, 2 ** 29, 0)
    order = jnp.argsort(score_values, axis=1, stable=True)
    return order[:, :SEGS].astype(jnp.int32)


def shard_levels(stream_key, extent, shards, low, high):
    def one(dim, parts):
        steps = jax.random.uniform(jax.random.fold_in(jax.random.fold_in(stream_key, 6), dim), (parts,), jnp.float32, low / len(shards), high / len(shards))
        return jnp.repeat(jnp.exp(steps), extent[dim] // parts).reshape((-1,) + (1,) * (len(extent) - dim - 1))

    level = one(*shards[0])
    for cut in shards[1:]:
        level = level * one(*cut)
    return level


def length_profile(number_of, total, reach, lean):
    loads = [(1 << 20) // math.isqrt(standing ** lean) + 1 for standing in range(2, number_of + 1)]
    spare, counts = total - reach - (number_of - 1), [1] * (number_of - 1)
    while spare > 0:
        movable = [i for i in range(number_of - 1) if counts[i] < reach]
        pool, left = sum([loads[i] for i in movable]), spare
        for i in movable:
            extra = min(reach - counts[i], max(1, left * loads[i] // pool), spare)
            counts[i] = counts[i] + extra
            spare = spare - extra
    return np.array([reach] + counts)


def uneven_parts(key, amount, total, most, lean):
    if amount == 2:
        one = jax.random.randint(key, (), max(1, total - most), min(most, total - 1) + 1)
        return jnp.stack([one, total - one])
    tallies = jnp.asarray(length_profile(amount, total, most, lean), jnp.int32)
    couples = (amount - 1) // 2
    donor, sink = tallies[1:1 + 2 * couples:2], tallies[2:2 + 2 * couples:2]
    margin = jnp.minimum(donor - 1, most - sink)
    moved = jax.random.randint(jax.random.fold_in(key, 1), (couples,), 0, 1 << 20) % (margin + 1)
    tallies = tallies.at[1:1 + 2 * couples:2].set(donor - moved).at[2:2 + 2 * couples:2].set(sink + moved)
    return tallies[jax.random.permutation(jax.random.fold_in(key, 2), amount)]


def bell_draw(stream_key, extent, deviation, bound, pieces=(), kind=jnp.bfloat16):
    drawn = deviation * jax.random.normal(stream_key, extent, jnp.float32)
    if pieces:
        drawn = drawn * shard_levels(stream_key, extent, pieces, -0.22, 0.18)
    return jnp.clip(drawn, -bound, bound).astype(kind)


def setup_inputs(seed: int = 0, part: int = 0) -> dict:
    arg_keys = jax.random.split(jax.random.key(seed), 11)
    part_splits = jax.random.split(jax.random.fold_in(arg_keys[10], part), 11)
    output_gradient = bell_draw(part_splits[0], (PACKED_TOKENS, JOINED_OUTPUTS), 1.0, 6.0, ((0, 4), (1, 4)))
    saved_layer_input = bell_draw(part_splits[1], (PACKED_TOKENS, MODEL_WIDTH), 1.0, 6.0, ((0, 4), (1, 4)))
    adapter_middle = bell_draw(part_splits[2], (PACKED_TOKENS, ADAPTER_RANK), 1.0, 6.0, ((0, 4),))
    frozen_weight = bell_draw(arg_keys[3], (MODEL_WIDTH, JOINED_OUTPUTS), JOINED_OUTPUTS ** -0.5, 0.046875, ((0, 4), (1, 4)))
    block_row_scale = jnp.clip(jnp.exp(math.log(4.0) - 2.7725887 * jax.random.uniform(arg_keys[4], (MODEL_WIDTH // BLK, JOINED_OUTPUTS), jnp.float32) ** shard_levels(arg_keys[4], (MODEL_WIDTH // BLK, JOINED_OUTPUTS), ((0, 4), (1, 4)), -0.2, 0.2)), 0.25, 4.0)
    adapter_down_weight = bell_draw(part_splits[5], (ADAPTER_COUNT, ADAPTER_RANK, MODEL_WIDTH), (4 * ADAPTER_RANK) ** -0.5, 0.375, ((2, 4),))
    adapter_up_weight = bell_draw(part_splits[6], (ADAPTER_COUNT, ADAPTER_RANK, JOINED_OUTPUTS), JOINED_OUTPUTS ** -0.5, 0.046875, ((2, 4),))
    document_lengths = jax.vmap(lambda own: uneven_parts(own, SEGS, TOKENS_PER_SHARD, MOST, 2))(jax.random.split(part_splits[7], N_DP)).reshape((N_DP, SEGS)).astype(jnp.int32)
    document_adapter = draw_document_adapter(jax.random.fold_in(jax.random.fold_in(arg_keys[10], part), 71), part)
    adapter_out_row = jax.random.permutation(part_splits[9], ADAPTER_COUNT).astype(jnp.int32)
    return {"output_gradient": output_gradient, "saved_layer_input": saved_layer_input, "adapter_middle": adapter_middle, "frozen_weight": frozen_weight, "block_row_scale": block_row_scale, "adapter_down_weight": adapter_down_weight, "adapter_up_weight": adapter_up_weight, "document_lengths": document_lengths, "document_adapter": document_adapter, "adapter_out_row": adapter_out_row}


adapter_gain = 2.0


def token_adapters(document_lengths, document_adapter, tok_dev):
    ends = jnp.cumsum(document_lengths, axis=1).astype(jnp.int32)
    starts = (ends - document_lengths).astype(jnp.int32)
    position = jnp.arange(tok_dev, dtype=jnp.int32)
    inside = (starts[:, :, None] <= position[None, None, :]) & (position[None, None, :] < ends[:, :, None])
    chosen = jnp.sum(jnp.where(inside, document_adapter[:, :, None], 0), axis=1)
    return chosen.reshape(-1).astype(jnp.int32)


def slot_lookup(labels, adapter_out_row):
    count = adapter_out_row.shape[0]
    match = labels[:, None] == jnp.arange(count, dtype=jnp.int32)[None, :]
    return jnp.sum(jnp.where(match, adapter_out_row[None, :], 0), axis=1).astype(jnp.int32)


def one_hot(labels, count):
    return (labels[:, None] == jnp.arange(count, dtype=jnp.int32)[None, :]).astype(jnp.bfloat16)


def spread_rows(selection, values):
    rows = values.shape[0]
    return (selection[:, :, None] * values[:, None, :]).reshape(rows, selection.shape[1] * values.shape[1])


def reference(output_gradient, saved_layer_input, adapter_middle, frozen_weight, block_row_scale, adapter_down_weight, adapter_up_weight, document_lengths, document_adapter, adapter_out_row):
    labels = token_adapters(document_lengths, document_adapter, TOKENS_PER_SHARD)
    slots = slot_lookup(labels, adapter_out_row)
    selection = one_hot(labels, ADAPTER_COUNT)
    flattened_up = adapter_up_weight.reshape(ADAPTER_COUNT * ADAPTER_RANK, JOINED_OUTPUTS)
    score_values = jnp.dot(output_gradient, flattened_up.T, preferred_element_type=jnp.float32).reshape(PACKED_TOKENS, ADAPTER_COUNT, ADAPTER_RANK)
    middle_gradient = (adapter_gain * jnp.sum(score_values * selection.astype(jnp.float32)[:, :, None], axis=1)).astype(jnp.bfloat16)

    width = JOINED_OUTPUTS // N_TENSOR

    def add_block(total, index):
        start = (index * width).astype(jnp.int32)
        columns = lax.dynamic_slice_in_dim(frozen_weight, start, width, 1)
        scales = jnp.repeat(lax.dynamic_slice_in_dim(block_row_scale, start, width, 1), BLK, axis=0)
        weight = (columns.astype(jnp.float32) * scales).astype(jnp.bfloat16)
        rows = lax.dynamic_slice_in_dim(output_gradient, start, width, 1)
        return total + jnp.dot(rows, weight.T, preferred_element_type=jnp.float32), None

    base_sum, _ = lax.scan(add_block, jnp.zeros((PACKED_TOKENS, MODEL_WIDTH), jnp.float32), jnp.arange(N_TENSOR, dtype=jnp.int32))
    adapter_contribution = jnp.dot(spread_rows(selection, middle_gradient), adapter_down_weight.reshape(ADAPTER_COUNT * ADAPTER_RANK, MODEL_WIDTH), preferred_element_type=jnp.float32)
    input_grad = (base_sum + adapter_contribution).astype(jnp.bfloat16)

    slot_selection = one_hot(slots, ADAPTER_COUNT)
    mid_spread = spread_rows(slot_selection, middle_gradient).reshape(N_DP, TOKENS_PER_SHARD, ADAPTER_COUNT * ADAPTER_RANK)
    stored_spread = spread_rows(slot_selection, adapter_middle).reshape(N_DP, TOKENS_PER_SHARD, ADAPTER_COUNT * ADAPTER_RANK)
    blocks = (mid_spread, stored_spread, saved_layer_input.reshape(N_DP, TOKENS_PER_SHARD, MODEL_WIDTH), output_gradient.reshape(N_DP, TOKENS_PER_SHARD, JOINED_OUTPUTS))

    def add_grads(totals, block):
        mid_block, stored_block, input_block, output_block = block
        down_part = jnp.dot(mid_block.T, input_block, preferred_element_type=jnp.float32).astype(jnp.bfloat16)
        up_portion = (adapter_gain * jnp.dot(stored_block.T, output_block, preferred_element_type=jnp.float32)).astype(jnp.bfloat16)
        down_part, up_portion = lax.optimization_barrier((down_part, up_portion))
        return (totals[0] + down_part.astype(jnp.float32), totals[1] + up_portion.astype(jnp.float32)), None

    start_totals = (jnp.zeros((ADAPTER_COUNT * ADAPTER_RANK, MODEL_WIDTH), jnp.float32), jnp.zeros((ADAPTER_COUNT * ADAPTER_RANK, JOINED_OUTPUTS), jnp.float32))
    (down_total, up_total), _ = lax.scan(add_grads, start_totals, blocks)
    return input_grad, down_total.reshape(ADAPTER_COUNT, ADAPTER_RANK, MODEL_WIDTH), up_total.reshape(ADAPTER_COUNT, ADAPTER_RANK, JOINED_OUTPUTS)
```

```python
import functools

import jax
import jax.numpy as jnp
from jax import lax
from jax.experimental import pallas as pl
from jax.experimental.pallas import tpu as pltpu
from jax.sharding import PartitionSpec as P

MESH = pl.DeviceIdType.MESH
BLK = 64
PIECE = 128
F32 = jnp.float32
BF16 = jnp.bfloat16


def spans(total, step):
    return [(s, min(step, total - s)) for s in range(0, total, step)]


def tiled(total, step, body):
    full = total // step

    def run(j, carry):
        body(pl.multiple_of(j * step, 128), step)
        return carry

    lax.fori_loop(0, full, run, 0)
    if total % step:
        body(full * step, total % step)


def dot_nt(a, b):
    return lax.dot_general(a, b, (((1,), (1,)), ((), ())), preferred_element_type=F32)


def fused(
    n,
    len_s, doc_s, row_s,
    g_h, x_h, mid_h, w_h, sc_h, dn_h, up_h,
    out_h, gd_h, gu_h,
    gall, w, sc, x, dn, up, mid, at, mpart, mrecv, sacc, acc, psend, precv, part, rsrecv, gu, gd,
    loc, wsem, ag_s, ag_r, a_s, a_r, m_s, m_r, rs_s, rs_r, p_s, p_r,
):
    z = lax.axis_index("dp")
    t = lax.axis_index("tensor")
    tok, kdim = g_h.shape
    ndim = x_h.shape[1]
    ranks = up_h.shape[0]
    rank = mid_h.shape[1]
    shift = rank.bit_length() - 1
    pieces = w_h.shape[0] // PIECE
    chunks = spans(kdim, 1024)

    loads = [
        pltpu.make_async_copy(src, dst, loc.at[i])
        for i, (src, dst) in enumerate(
            [(g_h, gall.at[z]), (up_h, up), (mid_h, mid), (sc_h, sc), (x_h, x), (dn_h, dn)]
        )
    ]
    for copy in loads:
        copy.start()

    def w_copy(i):
        rows = pl.ds(pl.multiple_of(i * PIECE, PIECE), PIECE)
        return pltpu.make_async_copy(w_h.at[rows], w.at[rows], wsem.at[i])

    def start_w(i, carry):
        w_copy(i).start()
        return carry

    lax.fori_loop(0, pieces, start_w, 0)

    barrier = pltpu.get_barrier_semaphore()
    for d in range(1, n):
        pl.semaphore_signal(barrier, inc=1, device_id={"dp": lax.rem(z + d, n)}, device_id_type=MESH)
        pl.semaphore_signal(barrier, inc=1, device_id={"tensor": lax.rem(t + d, n)}, device_id_type=MESH)
    pl.semaphore_wait(barrier, 2 * (n - 1))

    def ag(direction, b, c):
        first, width = chunks[c]
        ref = gall.at[b, :, pl.ds(first, width)]
        return pltpu.make_async_remote_copy(
            src_ref=ref,
            dst_ref=ref,
            send_sem=ag_s.at[direction, b, c],
            recv_sem=ag_r.at[b, c],
            device_id={"dp": z + 1 if direction == 0 else z - 1},
            device_id_type=MESH,
        )

    loads[0].wait()
    for c in range(len(chunks)):

        @pl.when(z < n - 1)
        def _():
            ag(0, z, c).start()

        @pl.when(z > 0)
        def _():
            ag(1, z, c).start()

    def doc_values(b, position, pick):
        total = jnp.zeros(position.shape, jnp.int32)
        begin = jnp.int32(0)
        for s in range(len_s.shape[1]):
            end = begin + len_s[b, s]
            inside = (position >= begin) & (position < end)
            total = total + jnp.where(inside, pick(b, s), 0)
            begin = end
        return total

    def adapter_of(b, s):
        return doc_s[b, s]

    def slot_of(b, s):
        a = doc_s[b, s]
        found = jnp.int32(0)
        for i in range(row_s.shape[0]):
            found = found + jnp.where(a == i, row_s[i], 0)
        return found

    row_id = lax.broadcasted_iota(jnp.int32, (tok, ranks), 0)
    col_group = lax.broadcasted_iota(jnp.int32, (tok, ranks), 1) >> shift

    def masked_scores(b, score):
        keep = doc_values(b, row_id, adapter_of) == col_group
        return jnp.where(keep, 2.0 * score, 0.0).astype(BF16)

    loads[2].wait()
    at[z] = mid[...].astype(F32).T.astype(BF16)

    def a_copy(d):
        return pltpu.make_async_remote_copy(
            src_ref=at.at[z],
            dst_ref=at.at[z],
            send_sem=a_s.at[d - 1],
            recv_sem=a_r.at[z],
            device_id={"dp": lax.rem(z + d, n)},
            device_id_type=MESH,
        )

    def a_wait(b):
        pltpu.make_async_remote_copy(
            src_ref=at.at[b], dst_ref=at.at[b], send_sem=a_s.at[0], recv_sem=a_r.at[b],
            device_id={"dp": lax.rem(z + 1, n)}, device_id_type=MESH,
        ).wait_recv()

    for d in range(1, n):
        a_copy(d).start()

    loads[1].wait()
    own_score = dot_nt(gall[z], up[...])
    mpart[...] = masked_scores(z, own_score)

    def m_copy(d):
        return pltpu.make_async_remote_copy(
            src_ref=mpart,
            dst_ref=mrecv.at[d - 1],
            send_sem=m_s.at[d - 1],
            recv_sem=m_r.at[d - 1],
            device_id={"tensor": lax.rem(t + d, n)},
            device_id_type=MESH,
        )

    for d in range(1, n):
        m_copy(d).start()

    loads[3].wait()

    def scale_w(i, carry):
        w_copy(i).wait()
        for h in range(PIECE // BLK):
            rows = pl.ds(pl.multiple_of(i * PIECE + h * BLK, BLK), BLK)
            for first, width in spans(kdim, 512):
                cols = pl.ds(first, width)
                factor = sc[pl.ds(i * (PIECE // BLK) + h, 1), cols]
                w[rows, cols] = (w[rows, cols].astype(F32) * factor).astype(BF16)
        return carry

    lax.fori_loop(0, pieces // 3, scale_w, 0)

    for d in range(1, n):
        m_copy(d).wait_recv()
    total = mpart[...].astype(F32)
    for d in range(1, n):
        total = total + mrecv[d - 1].astype(F32)
    same = (
        lax.broadcasted_iota(jnp.int32, (ranks, ranks), 0) & (rank - 1)
    ) == (lax.broadcasted_iota(jnp.int32, (ranks, ranks), 1) & (rank - 1))
    copies = jnp.dot(
        total.astype(BF16), jnp.where(same, 1.0, 0.0).astype(BF16), preferred_element_type=F32
    )
    slot_mask = doc_values(z, row_id, slot_of) == col_group
    by_slot = jnp.where(slot_mask, copies, 0.0).T.astype(BF16)
    loads[4].wait()

    def down_tile(first, width):
        cols = pl.ds(first, width)
        value = jnp.dot(by_slot, x[:, cols], preferred_element_type=F32).astype(BF16)
        for k in range(n):
            part[k, :, cols] = value[k * rank:(k + 1) * rank]

    tiled(ndim, 512, down_tile)

    def rs(direction, k):
        if direction == 0:
            place, target = k, z + 1
        else:
            place, target = jnp.where(k == z - 1, n, k), z - 1
        return pltpu.make_async_remote_copy(
            src_ref=part.at[k],
            dst_ref=rsrecv.at[place],
            send_sem=rs_s.at[k],
            recv_sem=rs_r.at[place],
            device_id={"dp": target},
            device_id_type=MESH,
        )

    def rs_wait(place):
        pltpu.make_async_remote_copy(
            src_ref=part.at[0], dst_ref=rsrecv.at[place], send_sem=rs_s.at[0],
            recv_sem=rs_r.at[place], device_id={"dp": lax.rem(z + 1, n)}, device_id_type=MESH,
        ).wait_recv()

    def rs_add(place, k):
        rs_wait(place)

        def add(first, width):
            cols = pl.ds(first, width)
            part[k, :, cols] = (
                part[k, :, cols].astype(F32) + rsrecv[place, :, cols].astype(F32)
            ).astype(BF16)

        tiled(ndim, 512, add)

    for k in range(n - 1, 0, -1):

        @pl.when(z == 0)
        def _():
            rs(0, k).start()

        @pl.when(z == n - 1)
        def _():
            rs(1, n - 1 - k).start()

    lax.fori_loop(pieces // 3, pieces, scale_w, 0)

    def multiply(b, c, lane):
        first, width = chunks[c]
        cols = pl.ds(first, width)
        rows = gall[b, :, cols]
        score = dot_nt(rows, up[:, cols])
        sacc[lane] = score if c == 0 else sacc[lane] + score

        def tile(begin, size):
            here = pl.ds(begin, size)
            value = dot_nt(rows, w[here, cols])
            acc[lane, :, here] = value if c == 0 else acc[lane, :, here] + value

        tiled(ndim, 512, tile)

    def p_copy(b):
        rel = lax.rem(t - b - 1 + 2 * n, n)
        return pltpu.make_async_remote_copy(
            src_ref=psend.at[b],
            dst_ref=precv.at[rel],
            send_sem=p_s.at[b],
            recv_sem=p_r.at[rel],
            device_id={"tensor": b},
            device_id_type=MESH,
        )

    def finish(b, lane):
        picked = masked_scores(b, sacc[lane])

        def tile(begin, size):
            here = pl.ds(begin, size)
            value = acc[lane, :, here] + jnp.dot(picked, dn[:, here], preferred_element_type=F32)
            psend[b, :, here] = value.astype(BF16)

        tiled(ndim, 512, tile)

        @pl.when(b != t)
        def _():
            p_copy(b).start()

    lane_id = lax.broadcasted_iota(jnp.int32, (rank, tok), 1)

    def up_terms(b, fresh):
        mine = doc_values(b, lane_id, slot_of) == z
        held = jnp.where(mine, 2.0 * at[b].astype(F32), 0.0).astype(BF16)

        def tile(begin, size):
            here = pl.ds(begin, size)
            value = jnp.dot(held, gall[b, :, here], preferred_element_type=F32)
            value = value.astype(BF16).astype(F32)
            gu[:, here] = value if fresh else gu[:, here] + value

        tiled(kdim, 512, tile)

    loads[5].wait()
    for c in range(len(chunks)):
        multiply(z, c, 0)
    finish(z, 0)
    up_terms(z, True)

    def round_step(s, carry):
        low, high = z - s, z + s
        for c in range(len(chunks)):

            @pl.when(low >= 0)
            def _():
                ag(0, low, c).wait_recv()

                @pl.when(z < n - 1)
                def _():
                    ag(0, low, c).start()

            @pl.when(high < n)
            def _():
                ag(1, high, c).wait_recv()

                @pl.when(z > 0)
                def _():
                    ag(1, high, c).start()

            @pl.when(low >= 0)
            def _():
                multiply(low, c, 0)

            @pl.when(high < n)
            def _():
                multiply(high, c, 1)

        @pl.when(low >= 0)
        def _():
            finish(low, 0)
            a_wait(low)
            up_terms(low, False)

        @pl.when(high < n)
        def _():
            finish(high, 1)
            a_wait(high)
            up_terms(high, False)

        up_slot = z + n - 1 - s

        @pl.when((z > 0) & (up_slot < n) & (up_slot > z))
        def _():
            rs_add(up_slot, up_slot)
            rs(0, up_slot).start()

        down_slot = z - (n - 1) + s

        @pl.when((z < n - 1) & (down_slot >= 0) & (down_slot < z))
        def _():
            rs_add(down_slot, down_slot)
            rs(1, down_slot).start()

        return carry

    lax.fori_loop(1, n, round_step, 0)
    write_up = pltpu.make_async_copy(gu, gu_h, loc.at[0])
    write_up.start()

    @pl.when(z > 0)
    def _():
        rs_wait(z)

    @pl.when(z < n - 1)
    def _():
        rs_wait(n)

    @pl.when(z == 0)
    def _():
        gd[...] = part[z].astype(F32) + rsrecv[n].astype(F32)

    @pl.when(z == n - 1)
    def _():
        gd[...] = part[z].astype(F32) + rsrecv[z].astype(F32)

    @pl.when((z > 0) & (z < n - 1))
    def _():
        gd[...] = part[z].astype(F32) + rsrecv[z].astype(F32) + rsrecv[n].astype(F32)

    write_down = pltpu.make_async_copy(gd, gd_h, loc.at[1])
    write_down.start()

    for rel in range(n - 1):
        pltpu.make_async_remote_copy(
            src_ref=psend.at[0], dst_ref=precv.at[rel], send_sem=p_s.at[0], recv_sem=p_r.at[rel],
            device_id={"tensor": lax.rem(t + 1, n)}, device_id_type=MESH,
        ).wait_recv()

    def out_tile(begin, size):
        here = pl.ds(begin, size)
        value = psend[t, :, here].astype(F32)
        for rel in range(n - 1):
            value = value + precv[rel, :, here].astype(F32)
        psend[t, :, here] = value.astype(BF16)

    tiled(ndim, 512, out_tile)
    write_out = pltpu.make_async_copy(psend.at[t], out_h, loc.at[2])
    write_out.start()

    for d in range(1, n):
        a_copy(d).wait_send()
        m_copy(d).wait_send()
    for b in range(n):
        for c in range(len(chunks)):

            @pl.when((z < n - 1) & (b <= z))
            def _():
                ag(0, b, c).wait_send()

            @pl.when((z > 0) & (b >= z))
            def _():
                ag(1, b, c).wait_send()

        @pl.when(b > z)
        def _():
            rs(0, b).wait_send()

        @pl.when(b < z)
        def _():
            rs(1, b).wait_send()

        @pl.when(b != t)
        def _():
            p_copy(b).wait_send()

    write_up.wait()
    write_down.wait()
    write_out.wait()


def fused_device(n, out_grad, saved, middle, weight, scale, down, up, lengths, adapters, rows):
    tok, kdim = out_grad.shape
    ndim = saved.shape[1]
    count, rank, _ = up.shape
    ranks = count * rank
    chunks = len(spans(kdim, 1024))
    smem = pl.BlockSpec(memory_space=pltpu.SMEM)
    hbm = pl.BlockSpec(memory_space=pl.ANY)
    dma = pltpu.SemaphoreType.DMA
    out, gd, gu = pl.pallas_call(
        functools.partial(fused, n),
        out_shape=(
            jax.ShapeDtypeStruct((tok, ndim), BF16),
            jax.ShapeDtypeStruct((rank, ndim), F32),
            jax.ShapeDtypeStruct((rank, kdim), F32),
        ),
        in_specs=[smem] * 3 + [hbm] * 7,
        out_specs=(hbm, hbm, hbm),
        scratch_shapes=[
            pltpu.VMEM((n, tok, kdim), BF16),
            pltpu.VMEM(weight.shape, BF16),
            pltpu.VMEM(scale.shape, F32),
            pltpu.VMEM((tok, ndim), BF16),
            pltpu.VMEM((ranks, ndim), BF16),
            pltpu.VMEM((ranks, kdim), BF16),
            pltpu.VMEM((tok, rank), BF16),
            pltpu.VMEM((n, rank, tok), BF16),
            pltpu.VMEM((tok, ranks), BF16),
            pltpu.VMEM((n - 1, tok, ranks), BF16),
            pltpu.VMEM((2, tok, ranks), F32),
            pltpu.VMEM((2, tok, ndim), F32),
            pltpu.VMEM((n, tok, ndim), BF16),
            pltpu.VMEM((n - 1, tok, ndim), BF16),
            pltpu.VMEM((n, rank, ndim), BF16),
            pltpu.VMEM((n + 1, rank, ndim), BF16),
            pltpu.VMEM((rank, kdim), F32),
            pltpu.VMEM((rank, ndim), F32),
            dma((6,)),
            dma((weight.shape[0] // PIECE,)),
            dma((2, n, chunks)),
            dma((n, chunks)),
            dma((n - 1,)),
            dma((n,)),
            dma((n - 1,)),
            dma((n - 1,)),
            dma((n,)),
            dma((n + 1,)),
            dma((n,)),
            dma((n - 1,)),
        ],
        compiler_params=pltpu.CompilerParams(
            collective_id=0, has_side_effects=True, vmem_limit_bytes=63 * 1024 * 1024
        ),
        cost_estimate=pl.CostEstimate(
            flops=2 * n * tok * kdim * ndim,
            bytes_accessed=2 * kdim * ndim,
            transcendentals=0,
        ),
        name="fused_backward",
    )(
        lengths, adapters, rows,
        out_grad, saved, middle, weight, scale,
        down.reshape(ranks, down.shape[2]), up.reshape(ranks, up.shape[2]),
    )
    return out, gd[None], gu[None]


adapter_gain = 2.0


def token_adapters(document_lengths, document_adapter, tok_dev):
    ends = jnp.cumsum(document_lengths, axis=1)
    starts = ends - document_lengths
    position = jnp.arange(tok_dev, dtype=jnp.int32)
    inside = (starts[:, :, None] <= position[None, None, :]) & (
        position[None, None, :] < ends[:, :, None]
    )
    chosen = jnp.sum(jnp.where(inside, document_adapter[:, :, None], 0), axis=1)
    return chosen.reshape(-1)


def slot_lookup(labels, adapter_out_row):
    count = adapter_out_row.shape[0]
    match = labels[:, None] == jnp.arange(count, dtype=jnp.int32)[None, :]
    return jnp.sum(jnp.where(match, adapter_out_row[None, :], 0), axis=1)


def one_hot(labels, count):
    return (labels[:, None] == jnp.arange(count, dtype=jnp.int32)[None, :]).astype(jnp.bfloat16)


def spread_rows(selection, values):
    rows = values.shape[0]
    return (selection[:, :, None] * values[:, None, :]).reshape(
        rows, selection.shape[1] * values.shape[1]
    )


def rank_terms(out_rows, flattened_up, selection, rank_position):
    score_values = jnp.einsum(
        "tn,kn->tk", out_rows, flattened_up, preferred_element_type=jnp.float32
    )
    score_values = score_values.reshape(out_rows.shape[0], selection.shape[1], rank_position)
    return adapter_gain * jnp.sum(score_values * selection.astype(jnp.float32)[:, :, None], axis=1)


def per_device(
    output_gradient,
    saved_layer_input,
    adapter_middle,
    frozen_weight,
    block_row_scale,
    adapter_down_weight,
    adapter_up_weight,
    document_lengths,
    document_adapter,
    adapter_out_row,
):
    tok_dev = output_gradient.shape[0]
    dp_index = lax.axis_index("dp")
    tp_index = lax.axis_index("tensor")
    tp_count = lax.axis_size("tensor")
    adapter_list = adapter_up_weight.shape[0]
    rank_position = adapter_up_weight.shape[1]
    labels = token_adapters(document_lengths, document_adapter, tok_dev)
    slots = slot_lookup(labels, adapter_out_row)
    selection = one_hot(labels, adapter_list)
    flattened_up = adapter_up_weight.reshape(
        adapter_list * rank_position, adapter_up_weight.shape[2]
    )
    scales = jnp.repeat(block_row_scale, BLK, axis=0)
    weight = (frozen_weight.astype(jnp.float32) * scales).astype(jnp.bfloat16)
    out_all = lax.all_gather(output_gradient, "dp", axis=0, tiled=True)
    all_terms = rank_terms(out_all, flattened_up, selection, rank_position)
    middle_gradient = lax.psum(all_terms.astype(jnp.bfloat16), "tensor")
    share = out_all.shape[0] // tp_count
    summed = lax.psum_scatter(
        jnp.einsum("tn,dn->td", out_all, weight, preferred_element_type=jnp.float32).astype(
            jnp.bfloat16
        ),
        "tensor",
        scatter_dimension=0,
        tiled=True,
    ).astype(jnp.float32)
    first_row = tp_index * share
    mid_rows_here = lax.dynamic_slice_in_dim(middle_gradient, first_row, share, 0)
    pick_rows = lax.dynamic_slice_in_dim(selection, first_row, share, 0)
    flattened_down = adapter_down_weight.reshape(
        adapter_list * rank_position, adapter_down_weight.shape[2]
    )
    adapter_contribution = jnp.dot(
        spread_rows(pick_rows, mid_rows_here), flattened_down, preferred_element_type=jnp.float32
    )
    input_grad = (summed + adapter_contribution).astype(jnp.bfloat16)
    own_slots = lax.dynamic_slice_in_dim(slots, dp_index * tok_dev, tok_dev, 0)
    own_mid = lax.dynamic_slice_in_dim(middle_gradient, dp_index * tok_dev, tok_dev, 0)
    slot_selection = one_hot(own_slots, adapter_list)
    down_part = jnp.einsum(
        "tk,td->kd",
        spread_rows(slot_selection, own_mid),
        saved_layer_input,
        preferred_element_type=jnp.float32,
    )
    up_portion = adapter_gain * jnp.einsum(
        "me,mr->er",
        spread_rows(slot_selection, adapter_middle),
        output_gradient,
        preferred_element_type=jnp.float32,
    )
    down_part = down_part.reshape(adapter_list, rank_position, -1)
    up_portion = up_portion.reshape(adapter_list, rank_position, -1)
    grad_down, grad_up = (
        lax.psum_scatter(
            down_part.astype(jnp.bfloat16), "dp", scatter_dimension=0, tiled=True
        ).astype(jnp.float32),
        lax.psum_scatter(
            up_portion.astype(jnp.bfloat16), "dp", scatter_dimension=0, tiled=True
        ).astype(jnp.float32),
    )
    return (input_grad, grad_down, grad_up)


def device_program(n_dp, n_tensor, *operands):
    out_grad, saved, middle, weight, _, _, up = operands[:7]
    tok, kdim = out_grad.shape
    count, rank, _ = up.shape
    whole_tiles = kdim % 128 == 0 and saved.shape[1] % 128 == 0 and tok % 128 == 0
    if (
        n_dp == n_tensor == count
        and whole_tiles
        and weight.shape == (saved.shape[1], kdim)
        and rank == 64
        and 2 * kdim * saved.shape[1] <= 32 * 1024 * 1024
    ):
        return fused_device(n_dp, *operands)
    return per_device(*operands)


def solution(mesh):
    placed = (
        P(("groups", "dp"), "tensor"),
        P(("groups", "dp"), "tensor"),
        P(("groups", "dp"), None),
        P("dp", "tensor"),
        P("dp", "tensor"),
        P("groups", None, "dp"),
        P("groups", None, "tensor"),
        P("groups", None),
        P("groups", None),
        P("groups"),
    )
    return jax.shard_map(
        functools.partial(device_program, mesh.shape["dp"], mesh.shape["tensor"]),
        mesh=mesh,
        in_specs=placed,
        out_specs=(
            P(("groups", "tensor"), "dp"),
            P(("groups", "dp"), None, "tensor"),
            P(("groups", "dp"), None, "tensor"),
        ),
        check_vma=False,
    )
```

```python
import functools

import jax
import jax.numpy as jnp
from jax import lax
from jax.experimental import pallas as pl
from jax.experimental.pallas import tpu as pltpu
from jax.sharding import PartitionSpec as P

MESH = pl.DeviceIdType.MESH
BLK = 64
PIECE = 128
F32 = jnp.float32
BF16 = jnp.bfloat16


def spans(total, step):
    return [(s, min(step, total - s)) for s in range(0, total, step)]


def tiled(total, step, body):
    full = total // step

    def run(j, carry):
        body(pl.multiple_of(j * step, 128), step)
        return carry

    lax.fori_loop(0, full, run, 0)
    if total % step:
        body(full * step, total % step)


def dot_nt(a, b):
    return lax.dot_general(a, b, (((1,), (1,)), ((), ())), preferred_element_type=F32)


def fused(
    n,
    len_s, doc_s, row_s,
    g_h, x_h, mid_h, w_h, sc_h, dn_h, up_h,
    out_h, gd_h, gu_h,
    gall, w, sc, x, dn, dnt, up, mid, at, mpart, mrecv, sacc, acc, psend, precv, part, rsrecv, gu, gd,
    loc, wsem, ag_s, ag_r, a_s, a_r, m_s, m_r, rs_s, rs_r, p_s, p_r,
):
    z = lax.axis_index("dp")
    t = lax.axis_index("tensor")
    tok, kdim = g_h.shape
    ndim = x_h.shape[1]
    ranks = up_h.shape[0]
    rank = mid_h.shape[1]
    shift = rank.bit_length() - 1
    pieces = w_h.shape[0] // PIECE
    chunks = spans(kdim, 1024)

    loads = [
        pltpu.make_async_copy(src, dst, loc.at[i])
        for i, (src, dst) in enumerate(
            [(g_h, gall.at[z]), (up_h, up), (mid_h, mid), (sc_h, sc), (x_h, x), (dn_h, dn)]
        )
    ]
    for copy in loads:
        copy.start()

    def w_copy(i):
        rows = pl.ds(pl.multiple_of(i * PIECE, PIECE), PIECE)
        return pltpu.make_async_copy(w_h.at[rows], w.at[rows], wsem.at[i])

    def start_w(i, carry):
        w_copy(i).start()
        return carry

    lax.fori_loop(0, pieces, start_w, 0)

    barrier = pltpu.get_barrier_semaphore()
    for d in range(1, n):
        pl.semaphore_signal(barrier, inc=1, device_id={"dp": lax.rem(z + d, n)}, device_id_type=MESH)
        pl.semaphore_signal(barrier, inc=1, device_id={"tensor": lax.rem(t + d, n)}, device_id_type=MESH)
    pl.semaphore_wait(barrier, 2 * (n - 1))

    def ag(direction, b, c):
        first, width = chunks[c]
        ref = gall.at[b, :, pl.ds(first, width)]
        return pltpu.make_async_remote_copy(
            src_ref=ref,
            dst_ref=ref,
            send_sem=ag_s.at[direction, b, c],
            recv_sem=ag_r.at[b, c],
            device_id={"dp": z + 1 if direction == 0 else z - 1},
            device_id_type=MESH,
        )

    near = t < n // 2
    early = len(chunks) // 2
    hold_up = (z == n - 2) & jnp.logical_not(near)
    hold_down = (z == 1) & near
    late = ((z == n - 1) & jnp.logical_not(near)) | ((z == 0) & near)

    loads[0].wait()
    for c in range(len(chunks)):
        now = c < early

        @pl.when((z < n - 1) & (jnp.logical_not(hold_up) | now))
        def _():
            ag(0, z, c).start()

        @pl.when((z > 0) & (jnp.logical_not(hold_down) | now))
        def _():
            ag(1, z, c).start()

    def doc_values(b, position, pick):
        total = jnp.zeros(position.shape, jnp.int32)
        begin = jnp.int32(0)
        for s in range(len_s.shape[1]):
            end = begin + len_s[b, s]
            inside = (position >= begin) & (position < end)
            total = total + jnp.where(inside, pick(b, s), 0)
            begin = end
        return total

    def adapter_of(b, s):
        return doc_s[b, s]

    def slot_of(b, s):
        a = doc_s[b, s]
        found = jnp.int32(0)
        for i in range(row_s.shape[0]):
            found = found + jnp.where(a == i, row_s[i], 0)
        return found

    row_id = lax.broadcasted_iota(jnp.int32, (tok, ranks), 0)
    col_group = lax.broadcasted_iota(jnp.int32, (tok, ranks), 1) >> shift

    def masked_scores(b, score):
        keep = doc_values(b, row_id, adapter_of) == col_group
        return jnp.where(keep, 2.0 * score, 0.0).astype(BF16)

    loads[2].wait()
    at[z] = mid[...].astype(F32).T.astype(BF16)

    def a_copy(d):
        return pltpu.make_async_remote_copy(
            src_ref=at.at[z],
            dst_ref=at.at[z],
            send_sem=a_s.at[d - 1],
            recv_sem=a_r.at[z],
            device_id={"dp": lax.rem(z + d, n)},
            device_id_type=MESH,
        )

    def a_wait(b):
        pltpu.make_async_remote_copy(
            src_ref=at.at[b], dst_ref=at.at[b], send_sem=a_s.at[0], recv_sem=a_r.at[b],
            device_id={"dp": lax.rem(z + 1, n)}, device_id_type=MESH,
        ).wait_recv()

    for d in range(1, n):
        a_copy(d).start()

    loads[1].wait()
    own_score = dot_nt(gall[z], up[...])
    mpart[...] = masked_scores(z, own_score)

    def m_copy(d):
        return pltpu.make_async_remote_copy(
            src_ref=mpart,
            dst_ref=mrecv.at[d - 1],
            send_sem=m_s.at[d - 1],
            recv_sem=m_r.at[d - 1],
            device_id={"tensor": lax.rem(t + d, n)},
            device_id_type=MESH,
        )

    for d in range(1, n):
        m_copy(d).start()

    loads[3].wait()

    def scale_w(i, carry):
        w_copy(i).wait()
        for h in range(PIECE // BLK):
            rows = pl.ds(pl.multiple_of(i * PIECE + h * BLK, BLK), BLK)
            for first, width in spans(kdim, 512):
                cols = pl.ds(first, width)
                factor = sc[pl.ds(i * (PIECE // BLK) + h, 1), cols]
                w[rows, cols] = (w[rows, cols].astype(F32) * factor).astype(BF16)
        return carry

    lax.fori_loop(0, pieces // 3, scale_w, 0)

    for d in range(1, n):
        m_copy(d).wait_recv()
    total = mpart[...].astype(F32)
    for d in range(1, n):
        total = total + mrecv[d - 1].astype(F32)
    same = (
        lax.broadcasted_iota(jnp.int32, (ranks, ranks), 0) & (rank - 1)
    ) == (lax.broadcasted_iota(jnp.int32, (ranks, ranks), 1) & (rank - 1))
    copies = jnp.dot(
        total.astype(BF16), jnp.where(same, 1.0, 0.0).astype(BF16), preferred_element_type=F32
    )
    slot_mask = doc_values(z, row_id, slot_of) == col_group
    by_slot = jnp.where(slot_mask, copies, 0.0).T.astype(BF16)
    loads[4].wait()

    def down_tile(first, width):
        cols = pl.ds(first, width)
        value = jnp.dot(by_slot, x[:, cols], preferred_element_type=F32).astype(BF16)
        for k in range(n):
            part[k, :, cols] = value[k * rank:(k + 1) * rank]

    tiled(ndim, 512, down_tile)

    def rs(direction, k):
        if direction == 0:
            place, target = k, z + 1
        else:
            place, target = jnp.where(k == z - 1, n, k), z - 1
        return pltpu.make_async_remote_copy(
            src_ref=part.at[k],
            dst_ref=rsrecv.at[place],
            send_sem=rs_s.at[k],
            recv_sem=rs_r.at[place],
            device_id={"dp": target},
            device_id_type=MESH,
        )

    def rs_wait(place):
        pltpu.make_async_remote_copy(
            src_ref=part.at[0], dst_ref=rsrecv.at[place], send_sem=rs_s.at[0],
            recv_sem=rs_r.at[place], device_id={"dp": lax.rem(z + 1, n)}, device_id_type=MESH,
        ).wait_recv()

    def rs_add(place, k):
        rs_wait(place)

        def add(first, width):
            cols = pl.ds(first, width)
            part[k, :, cols] = (
                part[k, :, cols].astype(F32) + rsrecv[place, :, cols].astype(F32)
            ).astype(BF16)

        tiled(ndim, 512, add)

    @pl.when(z == 0)
    def _():
        rs(0, n - 1).start()

    @pl.when(z == n - 1)
    def _():
        rs(1, 0).start()

    lax.fori_loop(pieces // 3, pieces, scale_w, 0)

    def multiply(b, c, lane):
        first, width = chunks[c]
        cols = pl.ds(first, width)
        rows = gall[b, :, cols]
        score = dot_nt(rows, up[:, cols])
        sacc[lane] = score if c == 0 else sacc[lane] + score

        def tile(begin, size):
            here = pl.ds(begin, size)
            value = dot_nt(w[here, cols], rows)
            acc[lane, here] = value if c == 0 else acc[lane, here] + value

        tiled(ndim, 1280, tile)

    def p_copy(b):
        rel = lax.rem(t - b - 1 + 2 * n, n)
        return pltpu.make_async_remote_copy(
            src_ref=psend.at[b],
            dst_ref=precv.at[rel],
            send_sem=p_s.at[b],
            recv_sem=p_r.at[rel],
            device_id={"tensor": b},
            device_id_type=MESH,
        )

    def finish(b, lane):
        picked = masked_scores(b, sacc[lane])

        def tile(begin, size):
            here = pl.ds(begin, size)
            psend[b, here] = (acc[lane, here] + dot_nt(dnt[here], picked)).astype(BF16)

        tiled(ndim, 512, tile)

        @pl.when(b != t)
        def _():
            p_copy(b).start()

    lane_id = lax.broadcasted_iota(jnp.int32, (rank, tok), 1)

    def up_terms(b, fresh):
        mine = doc_values(b, lane_id, slot_of) == z
        held = jnp.where(mine, 2.0 * at[b].astype(F32), 0.0).astype(BF16)

        def tile(begin, size):
            here = pl.ds(begin, size)
            value = jnp.dot(held, gall[b, :, here], preferred_element_type=F32)
            value = value.astype(BF16).astype(F32)
            gu[:, here] = value if fresh else gu[:, here] + value

        tiled(kdim, 512, tile)

    loads[5].wait()

    def turn(i, carry):
        here = pl.ds(pl.multiple_of(i * 128, 128), 128)
        dnt[here] = dn[:, here].astype(F32).T.astype(BF16)
        return carry

    lax.fori_loop(0, ndim // 128, turn, 0)
    for c in range(len(chunks)):
        multiply(z, c, 0)
    finish(z, 0)
    up_terms(z, True)

    def chunk_step(s, c, lane_low, lane_high):
        low, high = z - s, z + s

        @pl.when(low >= 0)
        def _():
            ag(0, low, c).wait_recv()

            @pl.when(z < n - 1)
            def _():
                ag(0, low, c).start()

        @pl.when(high < n)
        def _():
            ag(1, high, c).wait_recv()

            @pl.when(z > 0)
            def _():
                ag(1, high, c).start()

        @pl.when(low >= 0)
        def _():
            multiply(low, c, lane_low)

        @pl.when(high < n)
        def _():
            multiply(high, c, lane_high)

    def close_step(s, lane_low, lane_high):
        low, high = z - s, z + s

        @pl.when(low >= 0)
        def _():
            finish(low, lane_low)
            a_wait(low)
            up_terms(low, False)

        @pl.when(high < n)
        def _():
            finish(high, lane_high)
            a_wait(high)
            up_terms(high, False)

    def round_step(s, carry):
        held = late & (s == 1)
        low_lane = jnp.where(held, 1, 0)
        high_lane = jnp.where(late & (s > 1), 0, 1)
        for c in range(early):
            chunk_step(s, c, low_lane, high_lane)

        @pl.when(jnp.logical_not(held))
        def _():
            for c in range(early, len(chunks)):
                chunk_step(s, c, low_lane, high_lane)
            close_step(s, low_lane, high_lane)

        @pl.when(hold_up & (s == n - 2))
        def _():
            for c in range(early, len(chunks)):
                ag(0, z, c).start()

        @pl.when(hold_down & (s == n - 2))
        def _():
            for c in range(early, len(chunks)):
                ag(1, z, c).start()

        up_slot = z + n - 1 - s

        @pl.when((up_slot < n) & (up_slot > z))
        def _():
            @pl.when(z > 0)
            def _():
                rs_add(up_slot, up_slot)

            rs(0, up_slot).start()

        down_slot = z - (n - 1) + s

        @pl.when((down_slot >= 0) & (down_slot < z))
        def _():
            @pl.when(z < n - 1)
            def _():
                rs_add(down_slot, down_slot)

            rs(1, down_slot).start()

        return carry

    lax.fori_loop(1, n, round_step, 0)

    @pl.when(late)
    def _():
        for c in range(early, len(chunks)):
            chunk_step(1, c, 1, 1)
        close_step(1, 1, 1)

    write_up = pltpu.make_async_copy(gu, gu_h, loc.at[0])
    write_up.start()

    @pl.when(z > 0)
    def _():
        rs_wait(z)

    @pl.when(z < n - 1)
    def _():
        rs_wait(n)

    @pl.when(z == 0)
    def _():
        gd[...] = part[z].astype(F32) + rsrecv[n].astype(F32)

    @pl.when(z == n - 1)
    def _():
        gd[...] = part[z].astype(F32) + rsrecv[z].astype(F32)

    @pl.when((z > 0) & (z < n - 1))
    def _():
        gd[...] = part[z].astype(F32) + rsrecv[z].astype(F32) + rsrecv[n].astype(F32)

    write_down = pltpu.make_async_copy(gd, gd_h, loc.at[1])
    write_down.start()

    for rel in range(n - 1):
        pltpu.make_async_remote_copy(
            src_ref=psend.at[0], dst_ref=precv.at[rel], send_sem=p_s.at[0], recv_sem=p_r.at[rel],
            device_id={"tensor": lax.rem(t + 1, n)}, device_id_type=MESH,
        ).wait_recv()

    def out_tile(begin, size):
        here = pl.ds(begin, size)
        value = psend[t, here].astype(F32)
        for rel in range(n - 1):
            value = value + precv[rel, here].astype(F32)
        psend[t, here] = value.astype(BF16)

    tiled(ndim, 512, out_tile)
    write_out = pltpu.make_async_copy(psend.at[t], out_h, loc.at[2])
    write_out.start()

    for d in range(1, n):
        a_copy(d).wait_send()
        m_copy(d).wait_send()
    for b in range(n):
        for c in range(len(chunks)):

            @pl.when((z < n - 1) & (b <= z))
            def _():
                ag(0, b, c).wait_send()

            @pl.when((z > 0) & (b >= z))
            def _():
                ag(1, b, c).wait_send()

        @pl.when(b > z)
        def _():
            rs(0, b).wait_send()

        @pl.when(b < z)
        def _():
            rs(1, b).wait_send()

        @pl.when(b != t)
        def _():
            p_copy(b).wait_send()

    write_up.wait()
    write_down.wait()
    write_out.wait()


def fused_device(n, out_grad, saved, middle, weight, scale, down, up, lengths, adapters, rows):
    tok, kdim = out_grad.shape
    ndim = saved.shape[1]
    count, rank, _ = up.shape
    ranks = count * rank
    chunks = len(spans(kdim, 1024))
    smem = pl.BlockSpec(memory_space=pltpu.SMEM)
    hbm = pl.BlockSpec(memory_space=pl.ANY)
    dma = pltpu.SemaphoreType.DMA
    out, gd, gu = pl.pallas_call(
        functools.partial(fused, n),
        out_shape=(
            jax.ShapeDtypeStruct((ndim, tok), BF16),
            jax.ShapeDtypeStruct((rank, ndim), F32),
            jax.ShapeDtypeStruct((rank, kdim), F32),
        ),
        in_specs=[smem] * 3 + [hbm] * 7,
        out_specs=(hbm, hbm, hbm),
        scratch_shapes=[
            pltpu.VMEM((n, tok, kdim), BF16),
            pltpu.VMEM(weight.shape, BF16),
            pltpu.VMEM(scale.shape, F32),
            pltpu.VMEM((tok, ndim), BF16),
            pltpu.VMEM((ranks, ndim), BF16),
            pltpu.VMEM((ndim, ranks), BF16),
            pltpu.VMEM((ranks, kdim), BF16),
            pltpu.VMEM((tok, rank), BF16),
            pltpu.VMEM((n, rank, tok), BF16),
            pltpu.VMEM((tok, ranks), BF16),
            pltpu.VMEM((n - 1, tok, ranks), BF16),
            pltpu.VMEM((2, tok, ranks), F32),
            pltpu.VMEM((2, ndim, tok), F32),
            pltpu.VMEM((n, ndim, tok), BF16),
            pltpu.VMEM((n - 1, ndim, tok), BF16),
            pltpu.VMEM((n, rank, ndim), BF16),
            pltpu.VMEM((n + 1, rank, ndim), BF16),
            pltpu.VMEM((rank, kdim), F32),
            pltpu.VMEM((rank, ndim), F32),
            dma((6,)),
            dma((weight.shape[0] // PIECE,)),
            dma((2, n, chunks)),
            dma((n, chunks)),
            dma((n - 1,)),
            dma((n,)),
            dma((n - 1,)),
            dma((n - 1,)),
            dma((n,)),
            dma((n + 1,)),
            dma((n,)),
            dma((n - 1,)),
        ],
        compiler_params=pltpu.CompilerParams(
            collective_id=0, has_side_effects=True, vmem_limit_bytes=63 * 1024 * 1024
        ),
        cost_estimate=pl.CostEstimate(
            flops=2 * n * tok * kdim * ndim,
            bytes_accessed=2 * kdim * ndim,
            transcendentals=0,
        ),
        name="fused_backward",
    )(
        lengths, adapters, rows,
        out_grad, saved, middle, weight, scale,
        down.reshape(ranks, down.shape[2]), up.reshape(ranks, up.shape[2]),
    )
    return out.T, gd[None], gu[None]


adapter_gain = 2.0


def token_adapters(document_lengths, document_adapter, tok_dev):
    ends = jnp.cumsum(document_lengths, axis=1)
    starts = ends - document_lengths
    position = jnp.arange(tok_dev, dtype=jnp.int32)
    inside = (starts[:, :, None] <= position[None, None, :]) & (
        position[None, None, :] < ends[:, :, None]
    )
    chosen = jnp.sum(jnp.where(inside, document_adapter[:, :, None], 0), axis=1)
    return chosen.reshape(-1)


def slot_lookup(labels, adapter_out_row):
    count = adapter_out_row.shape[0]
    match = labels[:, None] == jnp.arange(count, dtype=jnp.int32)[None, :]
    return jnp.sum(jnp.where(match, adapter_out_row[None, :], 0), axis=1)


def one_hot(labels, count):
    return (labels[:, None] == jnp.arange(count, dtype=jnp.int32)[None, :]).astype(jnp.bfloat16)


def spread_rows(selection, values):
    rows = values.shape[0]
    return (selection[:, :, None] * values[:, None, :]).reshape(
        rows, selection.shape[1] * values.shape[1]
    )


def rank_terms(out_rows, flattened_up, selection, rank_position):
    score_values = jnp.einsum(
        "tn,kn->tk", out_rows, flattened_up, preferred_element_type=jnp.float32
    )
    score_values = score_values.reshape(out_rows.shape[0], selection.shape[1], rank_position)
    return adapter_gain * jnp.sum(score_values * selection.astype(jnp.float32)[:, :, None], axis=1)


def per_device(
    output_gradient,
    saved_layer_input,
    adapter_middle,
    frozen_weight,
    block_row_scale,
    adapter_down_weight,
    adapter_up_weight,
    document_lengths,
    document_adapter,
    adapter_out_row,
):
    tok_dev = output_gradient.shape[0]
    dp_index = lax.axis_index("dp")
    tp_index = lax.axis_index("tensor")
    tp_count = lax.axis_size("tensor")
    adapter_list = adapter_up_weight.shape[0]
    rank_position = adapter_up_weight.shape[1]
    labels = token_adapters(document_lengths, document_adapter, tok_dev)
    slots = slot_lookup(labels, adapter_out_row)
    selection = one_hot(labels, adapter_list)
    flattened_up = adapter_up_weight.reshape(
        adapter_list * rank_position, adapter_up_weight.shape[2]
    )
    scales = jnp.repeat(block_row_scale, BLK, axis=0)
    weight = (frozen_weight.astype(jnp.float32) * scales).astype(jnp.bfloat16)
    out_all = lax.all_gather(output_gradient, "dp", axis=0, tiled=True)
    all_terms = rank_terms(out_all, flattened_up, selection, rank_position)
    middle_gradient = lax.psum(all_terms.astype(jnp.bfloat16), "tensor")
    share = out_all.shape[0] // tp_count
    summed = lax.psum_scatter(
        jnp.einsum("tn,dn->td", out_all, weight, preferred_element_type=jnp.float32).astype(
            jnp.bfloat16
        ),
        "tensor",
        scatter_dimension=0,
        tiled=True,
    ).astype(jnp.float32)
    first_row = tp_index * share
    mid_rows_here = lax.dynamic_slice_in_dim(middle_gradient, first_row, share, 0)
    pick_rows = lax.dynamic_slice_in_dim(selection, first_row, share, 0)
    flattened_down = adapter_down_weight.reshape(
        adapter_list * rank_position, adapter_down_weight.shape[2]
    )
    adapter_contribution = jnp.dot(
        spread_rows(pick_rows, mid_rows_here), flattened_down, preferred_element_type=jnp.float32
    )
    input_grad = (summed + adapter_contribution).astype(jnp.bfloat16)
    own_slots = lax.dynamic_slice_in_dim(slots, dp_index * tok_dev, tok_dev, 0)
    own_mid = lax.dynamic_slice_in_dim(middle_gradient, dp_index * tok_dev, tok_dev, 0)
    slot_selection = one_hot(own_slots, adapter_list)
    down_part = jnp.einsum(
        "tk,td->kd",
        spread_rows(slot_selection, own_mid),
        saved_layer_input,
        preferred_element_type=jnp.float32,
    )
    up_portion = adapter_gain * jnp.einsum(
        "me,mr->er",
        spread_rows(slot_selection, adapter_middle),
        output_gradient,
        preferred_element_type=jnp.float32,
    )
    down_part = down_part.reshape(adapter_list, rank_position, -1)
    up_portion = up_portion.reshape(adapter_list, rank_position, -1)
    grad_down, grad_up = (
        lax.psum_scatter(
            down_part.astype(jnp.bfloat16), "dp", scatter_dimension=0, tiled=True
        ).astype(jnp.float32),
        lax.psum_scatter(
            up_portion.astype(jnp.bfloat16), "dp", scatter_dimension=0, tiled=True
        ).astype(jnp.float32),
    )
    return (input_grad, grad_down, grad_up)


def device_program(n_dp, n_tensor, *operands):
    out_grad, saved, middle, weight, _, _, up = operands[:7]
    tok, kdim = out_grad.shape
    count, rank, _ = up.shape
    whole_tiles = kdim % 128 == 0 and saved.shape[1] % 128 == 0 and tok % 128 == 0
    if (
        n_dp == n_tensor == count
        and whole_tiles
        and weight.shape == (saved.shape[1], kdim)
        and rank == 64
        and 2 * kdim * saved.shape[1] <= 32 * 1024 * 1024
    ):
        return fused_device(n_dp, *operands)
    return per_device(*operands)


def solution(mesh):
    placed = (
        P(("groups", "dp"), "tensor"),
        P(("groups", "dp"), "tensor"),
        P(("groups", "dp"), None),
        P("dp", "tensor"),
        P("dp", "tensor"),
        P("groups", None, "dp"),
        P("groups", None, "tensor"),
        P("groups", None),
        P("groups", None),
        P("groups"),
    )
    return jax.shard_map(
        functools.partial(device_program, mesh.shape["dp"], mesh.shape["tensor"]),
        mesh=mesh,
        in_specs=placed,
        out_specs=(
            P(("groups", "tensor"), "dp"),
            P(("groups", "dp"), None, "tensor"),
            P(("groups", "dp"), None, "tensor"),
        ),
        check_vma=False,
    )
```
